1024 devices in a mesh: gx: 16 (over z), gy: 4 (over x), gz: 16 (over y, core).
Axes of the slice: x: 4, y: 8, z: 16, core: 2. Of those that a mesh axis runs over, the one named last changes fastest.
Arguments:
- right_side: float32 [16, 4, 16, 2, 256], P('gx', 'gy', 'gz'), may hold values from -6 to 6
- hardness: float32 [16, 4, 16, 256], P('gx', 'gy', 'gz'), may hold values from 3 to 8
- coupling: bfloat16 [16, 4, 16, 6, 256, 256], P('gx', 'gy', 'gz'), may hold values from -0.078125 to 0.078125
- coupling_cols: int32 [16, 4, 16, 6], P('gx', 'gy', 'gz'), may hold values from 0 to 26, as said below
- coupling_count: int32 [16, 4, 16], P('gx', 'gy', 'gz'), may hold values from 2 to 6, as said below
- precond_diag: float32 [16, 4, 16, 256], P('gx', 'gy', 'gz'), may hold values from 0.5 to 1.5
- precond: bfloat16 [16, 4, 16, 6, 256, 256], P('gx', 'gy', 'gz'), may hold values from -0.01953125 to 0.01953125
- precond_cols: int32 [16, 4, 16, 6], P('gx', 'gy', 'gz'), may hold values from 0 to 26, as said below
Outputs:
- charges: float32 [16, 4, 16, 2, 256], P('gx', 'gy', 'gz')
- residual: float32 [16, 4, 16, 2, 256], P('gx', 'gy', 'gz')
The draws below stay inside these ranges and needn't reach their ends.
Inputs may be any that keep to these rules, and one draw needn't show every extreme that they name: `coupling_cols`: each block row's codes are distinct, and slot 0 is always 13, the block itself. `precond_cols`: each block row's codes are distinct, and slot 0 is always 13, the block itself. `coupling_count`: some block row has all 6 slots live.
All inputs are finite; a program needn't handle non-finite values.
Results may differ from the reference program's by a relative error of at most 0.0015.
Values may be sent and summed in bfloat16 or wider, within the bound.
A program may use at most 32 MiB of HBM per device.

```python
import math
import jax
import jax.numpy as jnp
from jax import lax

BS = 256
KH = 6
KG = 6
ITERS = 2
NX = 16
NY = 4
NZ = 16


def neighbour_codes(key, slots):
    keys = jax.random.split(key, NX * NY * NZ)
    perms = jax.vmap(lambda single: jax.random.permutation(single, 26))(keys)
    others = perms[:, :slots - 1]
    others = others + (others >= 13).astype(jnp.int32)
    selfcode = jnp.full((NX * NY * NZ, 1), 13, jnp.int32)
    return jnp.concatenate([selfcode, others.astype(jnp.int32)], axis=1).reshape(NX, NY, NZ, slots)


def draw_coupling_cols(key, part):
    key = jax.random.fold_in(key, 11)
    return neighbour_codes(key, KH)


def draw_precond_cols(key, part):
    key = jax.random.fold_in(key, 23)
    return neighbour_codes(key, KG)


def draw_coupling_count(key, part):
    key = jax.random.fold_in(key, 37)
    counts = jax.random.randint(key, (NX, NY, NZ), 2, KH + 1).astype(jnp.int32)
    counts = counts.at[0, 0, 0].set(KH)
    return counts.at[0, 0, NZ - 1].set(2)


def steps_of(stream_key, dims, shards, low, high):
    level = 1.0
    for position, shards_of in shards:
        draws = jax.random.uniform(jax.random.fold_in(jax.random.fold_in(stream_key, 6), position), (shards_of,), jnp.float32, low / len(shards), high / len(shards))
        level = level * jnp.repeat(jnp.exp(draws), dims[position] // shards_of).reshape((-1,) + (1,) * (len(dims) - 1 - position))
    return level


def scatter_about(key, shape, width, bound, shards=(), dtype=jnp.bfloat16):
    entries = jax.random.normal(key, shape, jnp.float32) * width
    if len(shards) > 0:
        entries = steps_of(key, shape, shards, -0.22, 0.18) * entries
    return jnp.clip(entries, min=-bound, max=bound).astype(dtype)


def setup_inputs(seed: int = 0) -> dict:
    streams_of = jax.random.split(jax.random.key(seed), 9)
    right_side = scatter_about(streams_of[0], (NX, NY, NZ, 2, BS), 1.0, 6.0, ((0, 16), (1, 4), (2, 16)), jnp.float32)
    hardness = jnp.clip(jnp.exp(math.log(8.0) - 0.98082925 * jax.random.uniform(streams_of[1], (NX, NY, NZ, BS), jnp.float32) ** steps_of(streams_of[1], (NX, NY, NZ, BS), ((0, 16), (1, 4), (2, 16)), -0.2, 0.2)), 3.0, 8.0)
    coupling = scatter_about(streams_of[2], (NX, NY, NZ, KH, BS, BS), (4 * BS * KH) ** -0.5, 0.078125, ((0, 16), (1, 4), (2, 16)))
    coupling_cols = draw_coupling_cols(jax.random.fold_in(streams_of[8], 71), 0)
    coupling_count = draw_coupling_count(jax.random.fold_in(streams_of[8], 71), 0)
    precond_diag = jnp.clip(jnp.exp(math.log(1.5) - 1.0986123 * jax.random.uniform(streams_of[5], (NX, NY, NZ, BS), jnp.float32) ** steps_of(streams_of[5], (NX, NY, NZ, BS), ((0, 16), (1, 4), (2, 16)), -0.2, 0.2)), 0.5, 1.5)
    precond = scatter_about(streams_of[6], (NX, NY, NZ, KG, BS, BS), (64 * BS * KG) ** -0.5, 0.01953125, ((0, 16), (1, 4), (2, 16)))
    precond_cols = draw_precond_cols(jax.random.fold_in(streams_of[8], 71), 0)
    return dict(right_side=right_side, hardness=hardness, coupling=coupling, coupling_cols=coupling_cols, coupling_count=coupling_count, precond_diag=precond_diag, precond=precond, precond_cols=precond_cols)


def column_index(cols):
    first = (jnp.arange(NX).reshape(NX, 1, 1, 1) + cols // 9 - 1) % NX
    second = (jnp.arange(NY).reshape(1, NY, 1, 1) + (cols // 3) % 3 - 1) % NY
    third = (jnp.arange(NZ).reshape(1, 1, NZ, 1) + cols % 3 - 1) % NZ
    return first, second, third


def forward_apply(tiles, cols, live, vecb):
    first, second, third = column_index(cols)
    picked = vecb[first, second, third].astype(jnp.float32) * live[..., None, None]

    def one_slab(pair):
        return jnp.einsum('yzkij,yzkrj->yzri', pair[0].astype(jnp.float32), pair[1])

    return lax.map(one_slab, (tiles, picked))


def backward_apply(tiles, cols, live, vecb):
    first, second, third = column_index(cols)

    def one_slab(pair):
        return jnp.einsum('yzkij,yzri->yzkrj', pair[0].astype(jnp.float32), pair[1].astype(jnp.float32))

    contrib = lax.map(one_slab, (tiles, vecb)) * live[..., None, None]
    return jnp.zeros((NX, NY, NZ, 2, BS), jnp.float32).at[first, second, third].add(contrib)


def inner(left, right):
    return jnp.sum(left * right, axis=(0, 1, 2, 4))


def reference(right_side, hardness, coupling, coupling_cols, coupling_count, precond_diag, precond, precond_cols):
    live_h = (jnp.arange(KH).reshape(1, 1, 1, KH) < coupling_count[..., None]).astype(jnp.float32)
    live_g = jnp.ones((NX, NY, NZ, KG), jnp.float32)
    diag_h = hardness[:, :, :, None, :]
    diag_g = precond_diag[:, :, :, None, :]

    def apply_h(vec):
        vecb = vec.astype(jnp.bfloat16)
        return diag_h * vec + forward_apply(coupling, coupling_cols, live_h, vecb) + backward_apply(coupling, coupling_cols, live_h, vecb)

    def apply_m(res):
        resb = res.astype(jnp.bfloat16)
        inter = diag_g * res + forward_apply(precond, precond_cols, live_g, resb)
        interb = inter.astype(jnp.bfloat16)
        return diag_g * inter + backward_apply(precond, precond_cols, live_g, interb)

    charges = jnp.zeros_like(right_side)
    residual = right_side
    zvec = apply_m(residual)
    direction = zvec
    rz_now = inner(residual, zvec)
    for step in range(ITERS):
        image = apply_h(direction)
        alpha = (rz_now / inner(direction, image))[:, None]
        charges = charges + alpha * direction
        residual = residual - alpha * image
        if step + 1 < ITERS:
            zvec = apply_m(residual)
            rz_next = inner(residual, zvec)
            direction = zvec + (rz_next / rz_now)[:, None] * direction
            rz_now = rz_next
    return charges, residual
```

```python
import jax
import jax.numpy as jnp
from jax import lax
from jax.experimental import pallas as pl
from jax.experimental.pallas import tpu as pltpu
from jax.sharding import PartitionSpec as P

SYS = 2
BS = 256
SLOTS = 6
CODES = 27
SELF = 13
AXES = ("gx", "gy", "gz")
MESH = pl.DeviceIdType.MESH
NEAR = sorted(
    (o for o in range(CODES) if o != SELF),
    key=lambda o: -(abs(o // 9 - 1) + abs(o // 3 % 3 - 1) + abs(o % 3 - 1)),
)


def dot_fwd(vec, tile):
    return lax.dot_general(vec, tile, (((1,), (1,)), ((), ())), preferred_element_type=jnp.float32)


def dot_bwd(vec, tile):
    return lax.dot_general(vec, tile, (((1,), (0,)), ((), ())), preferred_element_type=jnp.float32)


def kernel(
    sizes,
    rhs_hbm, hard_hbm, coup_hbm, ccol_hbm, ccnt_hbm, pdia_hbm, prec_hbm, pcol_hbm,
    charges_hbm, resid_hbm,
    rhs, hard, coup, pdia, prec, ccol, ccnt, pcol,
    inv_g, inv_h, sel_h,
    halo_a, send_b, fold_b, send_c, both_c, send_d, halo_d, send_e, fold_e, send_f, both_f,
    parts, part_gx, part_gz, part_gy, sums_x, sums_z,
    terms, out_c, out_r,
    load_sem, send_sem, recv_sem,
):
    me = [lax.axis_index(a) for a in AXES]
    steps = [
        [lax.rem(me[a] + (n - 1), n), me[a], lax.rem(me[a] + 1, n)] for a, n in enumerate(sizes)
    ]

    def near(code):
        return (steps[0][code // 9], steps[1][code // 3 % 3], steps[2][code % 3])

    def along(axis, distance):
        place = list(me)
        place[axis] = lax.rem(me[axis] + distance, sizes[axis])
        return tuple(place)

    loads = [
        pltpu.make_async_copy(source, target, load_sem.at[i])
        for i, (source, target) in enumerate((
            (rhs_hbm, rhs), (pcol_hbm, pcol), (ccol_hbm, ccol), (ccnt_hbm, ccnt), (pdia_hbm, pdia),
            (prec_hbm, prec), (hard_hbm, hard), (coup_hbm, coup),
        ))
    ]
    for load in loads:
        load.start()

    barrier = pltpu.get_barrier_semaphore()
    partners = 0
    for axis, n in enumerate(sizes):
        for distance in range(2, n - 1):
            pl.semaphore_signal(barrier, inc=1, device_id=along(axis, distance), device_id_type=MESH)
            partners += 1
    for code in NEAR:
        pl.semaphore_signal(barrier, inc=1, device_id=near(code), device_id_type=MESH)
        partners += 1

    zero = jnp.zeros((SYS, BS), jnp.float32)
    terms[SLOTS] = zero
    both_c[CODES, 0:SYS] = zero
    both_f[CODES, 0:SYS] = zero

    for load in loads[:4]:
        load.wait()
    halo_a[SELF] = rhs[...]
    codes_g = [pcol[0, k] for k in range(SLOTS)]
    count = ccnt[0, 0]
    codes_h = [ccol[0, k] for k in range(SLOTS)]
    for k in range(SLOTS):
        sel_h[k] = jnp.where(k < count, codes_h[k], CODES)
    codes_h = [sel_h[k] for k in range(SLOTS)]
    for inv, codes in ((inv_g, codes_g), (inv_h, codes_h)):
        for code in NEAR:
            slot = jnp.int32(SLOTS)
            for k in range(1, SLOTS):
                slot = jnp.where(codes[k] == code, k, slot)
            inv[code] = slot

    pl.semaphore_wait(barrier, partners)

    def exchange(phase, source_of, target):
        for code in NEAR:
            pltpu.make_async_remote_copy(
                src_ref=source_of(code),
                dst_ref=target.at[CODES - 1 - code],
                send_sem=send_sem.at[phase],
                recv_sem=recv_sem.at[phase],
                device_id=near(code),
                device_id_type=MESH,
            ).start()

    def arrived(phase, target, n):
        here = target.at[pl.ds(0, n)]
        pltpu.make_async_copy(here, here, recv_sem.at[phase]).wait()

    def left(phase, target, n):
        here = target.at[pl.ds(0, n)]
        pltpu.make_async_copy(here, here, send_sem.at[phase]).wait()

    def forward(tiles, codes, halo, rows):
        total = None
        for k in range(SLOTS):
            picked = halo[SELF, rows] if k == 0 else halo[codes[k], rows]
            term = dot_fwd(picked.astype(jnp.bfloat16), tiles[k])
            total = term if total is None else total + term
        return total

    def backward(tiles, vecb):
        own = dot_bwd(vecb, tiles[0])
        for k in range(1, SLOTS):
            terms[k] = dot_bwd(vecb, tiles[k])
        return own

    def folded(fold, rows):
        total = None
        for code in NEAR:
            term = fold[code, rows]
            total = term if total is None else total + term
        return total

    def inner(left_vec, right_vec):
        return jnp.sum(left_vec * right_vec, axis=1, keepdims=True)

    everything = slice(0, SYS)
    second = slice(SYS, 2 * SYS)

    def apply_m_tail(vec, halo, send, fold, phase):
        inter = pdia[...] * vec + forward(prec, codes_g, halo, everything)
        own = backward(prec, inter.astype(jnp.bfloat16))
        for code in NEAR:
            send[code] = terms[inv_g[code]]
        exchange(phase, lambda code: send.at[code], fold)
        partial = pdia[...] * inter + own
        arrived(phase, fold, CODES - 1)
        return partial + folded(fold, everything)

    def apply_h(vec, send, both, phase):
        own = backward(coup, vec.astype(jnp.bfloat16))
        for code in NEAR:
            send[code, everything] = vec
            send[code, second] = terms[inv_h[code]]
        exchange(phase, lambda code: send.at[code], both)
        both[SELF, everything] = vec
        partial = hard[...] * vec + own
        arrived(phase, both, CODES - 1)
        return partial + folded(both, second) + forward(coup, codes_h, both, everything)

    r0 = rhs[...]
    exchange(0, lambda code: rhs, halo_a)
    for load in loads[4:6]:
        load.wait()
    arrived(0, halo_a, CODES - 1)
    z0 = apply_m_tail(r0, halo_a, send_b, fold_b, 1)
    for load in loads[6:]:
        load.wait()
    w0 = apply_h(z0, send_c, both_c, 2)
    send_d[...] = w0
    halo_d[SELF] = w0
    exchange(3, lambda code: send_d, halo_d)
    lane = lax.broadcasted_iota(jnp.int32, (SYS, 128), 1)

    def placed(pairs):
        total = jnp.zeros((SYS, 128), jnp.float32)
        for place, value in pairs:
            total = jnp.where(lane == place, value, total)
        return total

    known = placed(((0, inner(r0, z0)), (1, inner(z0, w0))))
    arrived(3, halo_d, CODES - 1)
    y0 = apply_m_tail(w0, halo_d, send_e, fold_e, 4)
    q0 = apply_h(y0, send_f, both_f, 5)
    known = jnp.where(lane == 2, inner(w0, y0), known)
    known = jnp.where(lane == 3, inner(r0, y0), known)
    known = jnp.where(lane == 4, inner(y0, q0), known)

    parts[...] = known
    source, total = parts, known
    for stage, (axis, slots) in enumerate(((0, part_gx), (2, part_gz), (1, part_gy))):
        n, phase = sizes[axis], 6 + stage
        for distance in range(1, n):
            pltpu.make_async_remote_copy(
                src_ref=source,
                dst_ref=slots.at[distance - 1],
                send_sem=send_sem.at[phase],
                recv_sem=recv_sem.at[phase],
                device_id=along(axis, distance),
                device_id_type=MESH,
            ).start()
        arrived(phase, slots, n - 1)
        for distance in range(1, n):
            total = total + slots[distance - 1]
        if stage < 2:
            source = (sums_x, sums_z)[stage]
            source[...] = total

    rz0, c0, wy, ry, yq = (total[:, i : i + 1] for i in range(5))
    alpha = rz0 / c0
    rz1 = rz0 - alpha * (ry + c0) + alpha * alpha * wy
    scale = 1.0 + rz1 / rz0
    c1 = scale * scale * c0 - 2.0 * alpha * scale * wy + alpha * alpha * yq
    alpha1 = rz1 / c1
    out_c[...] = alpha * z0 + alpha1 * (scale * z0 - alpha * y0)
    out_r[...] = r0 - alpha * w0 - alpha1 * (scale * w0 - alpha * q0)
    outs = [
        pltpu.make_async_copy(out_c, charges_hbm, load_sem.at[0]),
        pltpu.make_async_copy(out_r, resid_hbm, load_sem.at[1]),
    ]
    for out in outs:
        out.start()
    for phase, target in ((0, halo_a), (1, fold_b), (2, both_c), (3, halo_d), (4, fold_e), (5, both_f)):
        left(phase, target, CODES - 1)
    for phase, target in ((6, part_gx), (7, part_gz), (8, part_gy)):
        left(phase, target, target.shape[0])
    for out in outs:
        out.wait()


def body(sizes, right_side, hardness, coupling, coupling_cols, coupling_count, precond_diag, precond, precond_cols):
    f32, i32, bf16 = jnp.float32, jnp.int32, jnp.bfloat16
    vec = jax.ShapeDtypeStruct((SYS, BS), f32)
    slots = lambda n, rows=SYS: pltpu.VMEM((n, rows, BS), f32)
    anywhere = pl.BlockSpec(memory_space=pl.ANY)

    def run(*refs):
        kernel(sizes, *refs)

    charges, residual = pl.pallas_call(
        run,
        out_shape=(vec, vec),
        in_specs=[anywhere] * 8,
        out_specs=(anywhere, anywhere),
        scratch_shapes=[
            pltpu.VMEM((SYS, BS), f32), pltpu.VMEM((1, BS), f32), pltpu.VMEM((SLOTS, BS, BS), bf16),
            pltpu.VMEM((1, BS), f32), pltpu.VMEM((SLOTS, BS, BS), bf16),
            pltpu.SMEM((1, SLOTS), i32), pltpu.SMEM((1, 1), i32), pltpu.SMEM((1, SLOTS), i32),
            pltpu.SMEM((CODES,), i32), pltpu.SMEM((CODES,), i32), pltpu.SMEM((SLOTS,), i32),
            slots(CODES), slots(CODES), slots(CODES), slots(CODES, 2 * SYS), slots(CODES + 1, 2 * SYS),
            pltpu.VMEM((SYS, BS), f32), slots(CODES), slots(CODES), slots(CODES), slots(CODES, 2 * SYS), slots(CODES + 1, 2 * SYS),
            pltpu.VMEM((SYS, 128), f32), pltpu.VMEM((sizes[0] - 1, SYS, 128), f32), pltpu.VMEM((sizes[2] - 1, SYS, 128), f32),
            pltpu.VMEM((sizes[1] - 1, SYS, 128), f32), pltpu.VMEM((SYS, 128), f32), pltpu.VMEM((SYS, 128), f32),
            slots(SLOTS + 1), pltpu.VMEM((SYS, BS), f32), pltpu.VMEM((SYS, BS), f32),
            pltpu.SemaphoreType.DMA((8,)), pltpu.SemaphoreType.DMA((9,)), pltpu.SemaphoreType.DMA((9,)),
        ],
        compiler_params=pltpu.CompilerParams(
            collective_id=0, has_side_effects=True, vmem_limit_bytes=32 * 1024 * 1024
        ),
    )(
        right_side.reshape(SYS, BS), hardness.reshape(1, BS), coupling.reshape(SLOTS, BS, BS),
        coupling_cols.reshape(1, SLOTS), coupling_count.reshape(1, 1), precond_diag.reshape(1, BS),
        precond.reshape(SLOTS, BS, BS), precond_cols.reshape(1, SLOTS),
    )
    return charges.reshape(right_side.shape), residual.reshape(right_side.shape)


def solution(mesh):
    sizes = tuple(mesh.shape[a] for a in AXES)
    placed = (
        P("gx", "gy", "gz", None, None),
        P("gx", "gy", "gz", None),
        P("gx", "gy", "gz", None, None, None),
        P("gx", "gy", "gz", None),
        P("gx", "gy", "gz"),
        P("gx", "gy", "gz", None),
        P("gx", "gy", "gz", None, None, None),
        P("gx", "gy", "gz", None),
    )
    return jax.shard_map(
        lambda *args: body(sizes, *args),
        mesh=mesh,
        in_specs=placed,
        out_specs=(P("gx", "gy", "gz", None, None), P("gx", "gy", "gz", None, None)),
        check_vma=False,
    )
```

```python
import jax
import jax.numpy as jnp
from jax import lax
from jax.experimental import pallas as pl
from jax.experimental.pallas import tpu as pltpu
from jax.sharding import PartitionSpec as P

SYS = 2
BS = 256
SLOTS = 6
CODES = 27
SELF = 13
AXES = ("gx", "gy", "gz")
MESH = pl.DeviceIdType.MESH
NEAR = sorted(
    (o for o in range(CODES) if o != SELF),
    key=lambda o: -(abs(o // 9 - 1) + abs(o // 3 % 3 - 1) + abs(o % 3 - 1)),
)


FURTHER = ((-2, 0, 0), (2, 0, 0), (0, 0, -2), (0, 0, 2))
SUMS = 5


def two_parts(vec):
    rest = vec - vec.astype(jnp.bfloat16).astype(jnp.float32)
    return jnp.concatenate([vec, rest], axis=0).astype(jnp.bfloat16)


def joined(product):
    return product[0:SYS] + product[SYS : 2 * SYS]


def dot_fwd(vec, tile):
    return lax.dot_general(vec, tile, (((1,), (1,)), ((), ())), preferred_element_type=jnp.float32)


def dot_bwd(vec, tile):
    return lax.dot_general(vec, tile, (((1,), (0,)), ((), ())), preferred_element_type=jnp.float32)


def kernel(
    sizes,
    rhs_hbm, hard_hbm, coup_hbm, ccol_hbm, ccnt_hbm, pdia_hbm, prec_hbm, pcol_hbm,
    charges, resid,
    rhs, hard, coup, pdia, prec, ccol, ccnt, pcol,
    inv_g, inv_h, sel_h,
    halo_a, send_b, fold_b, send_c, both_c, send_d, halo_d, send_e, fold_e, send_f, both_f,
    parts, part_plane, part_ring, sums_plane,
    terms,
    load_sem, send_sem, recv_sem,
):
    me = [lax.axis_index(a) for a in AXES]
    steps = [
        [lax.rem(me[a] + (n - 1), n), me[a], lax.rem(me[a] + 1, n)] for a, n in enumerate(sizes)
    ]

    def near(code):
        return (steps[0][code // 9], steps[1][code // 3 % 3], steps[2][code % 3])

    def away(distances):
        return tuple(
            m if d == 0 else lax.rem(m + d % n, n) for m, d, n in zip(me, distances, sizes)
        )

    loads = [
        pltpu.make_async_copy(source, target, load_sem.at[i])
        for i, (source, target) in enumerate((
            (rhs_hbm, rhs), (pcol_hbm, pcol), (ccol_hbm, ccol), (ccnt_hbm, ccnt), (pdia_hbm, pdia),
            (prec_hbm, prec), (hard_hbm, hard), (coup_hbm, coup),
        ))
    ]
    for load in loads:
        load.start()

    barrier = pltpu.get_barrier_semaphore()
    for code in NEAR:
        pl.semaphore_signal(barrier, inc=1, device_id=near(code), device_id_type=MESH)
    for distances in FURTHER:
        pl.semaphore_signal(barrier, inc=1, device_id=away(distances), device_id_type=MESH)

    zero = jnp.zeros((SYS, BS), jnp.float32)
    terms[SLOTS] = zero
    both_c[CODES, 0:SYS] = zero
    both_f[CODES, 0:SYS] = zero

    for load in loads[:4]:
        load.wait()
    halo_a[SELF] = rhs[...]
    codes_g = [pcol[0, k] for k in range(SLOTS)]
    count = ccnt[0, 0, 0]
    codes_h = [ccol[0, k] for k in range(SLOTS)]
    for k in range(SLOTS):
        sel_h[k] = jnp.where(k < count, codes_h[k], CODES)
    codes_h = [sel_h[k] for k in range(SLOTS)]
    for inv, codes in ((inv_g, codes_g), (inv_h, codes_h)):
        for code in NEAR:
            slot = jnp.int32(SLOTS)
            for k in range(1, SLOTS):
                slot = jnp.where(codes[k] == code, k, slot)
            inv[code] = slot

    pl.semaphore_wait(barrier, len(NEAR) + len(FURTHER))

    def exchange(phase, source_of, target):
        for code in NEAR:
            pltpu.make_async_remote_copy(
                src_ref=source_of(code),
                dst_ref=target.at[CODES - 1 - code],
                send_sem=send_sem.at[phase],
                recv_sem=recv_sem.at[phase],
                device_id=near(code),
                device_id_type=MESH,
            ).start()

    def arrived(phase, target, n):
        here = target.at[pl.ds(0, n)]
        pltpu.make_async_copy(here, here, recv_sem.at[phase]).wait()

    def left(phase, target, n):
        here = target.at[pl.ds(0, n)]
        pltpu.make_async_copy(here, here, send_sem.at[phase]).wait()

    def forward(tiles, codes, halo, rows):
        total = None
        for k in range(SLOTS):
            picked = halo[SELF, rows] if k == 0 else halo[codes[k], rows]
            term = dot_fwd(two_parts(picked), tiles[k])
            total = term if total is None else total + term
        return joined(total)

    def backward(tiles, vec):
        pair = two_parts(vec)
        for k in range(1, SLOTS):
            terms[k] = joined(dot_bwd(pair, tiles[k]))
        return joined(dot_bwd(pair, tiles[0]))

    def folded(fold, rows):
        total = None
        for code in NEAR:
            term = fold[code, rows]
            total = term if total is None else total + term
        return total

    def inner(left_vec, right_vec):
        return jnp.sum(left_vec * right_vec, axis=1, keepdims=True)

    everything = slice(0, SYS)
    second = slice(SYS, 2 * SYS)

    def apply_m_tail(vec, halo, send, fold, phase):
        inter = pdia[...] * vec + forward(prec, codes_g, halo, everything)
        own = backward(prec, inter)
        for code in NEAR:
            send[code] = terms[inv_g[code]]
        exchange(phase, lambda code: send.at[code], fold)
        partial = pdia[...] * inter + own
        arrived(phase, fold, CODES - 1)
        return partial + folded(fold, everything)

    def apply_h(vec, send, both, phase):
        own = backward(coup, vec)
        for code in NEAR:
            send[code, everything] = vec
            send[code, second] = terms[inv_h[code]]
        exchange(phase, lambda code: send.at[code], both)
        both[SELF, everything] = vec
        partial = hard[...] * vec + own
        arrived(phase, both, CODES - 1)
        return partial + folded(both, second) + forward(coup, codes_h, both, everything)

    r0 = rhs[...]
    exchange(0, lambda code: rhs, halo_a)
    for load in loads[4:6]:
        load.wait()
    arrived(0, halo_a, CODES - 1)
    z0 = apply_m_tail(r0, halo_a, send_b, fold_b, 1)
    for load in loads[6:]:
        load.wait()
    w0 = apply_h(z0, send_c, both_c, 2)
    send_d[...] = w0
    halo_d[SELF] = w0
    exchange(3, lambda code: send_d, halo_d)
    lane = lax.broadcasted_iota(jnp.int32, (1, 128), 1)

    def placed(row, place, value):
        row = jnp.where(lane == 2 * place, value[0:1], row)
        return jnp.where(lane == 2 * place + 1, value[1:2], row)

    known = placed(jnp.zeros((1, 128), jnp.float32), 0, inner(r0, z0))
    known = placed(known, 1, inner(z0, w0))
    arrived(3, halo_d, CODES - 1)
    y0 = apply_m_tail(w0, halo_d, send_e, fold_e, 4)
    q0 = apply_h(y0, send_f, both_f, 5)
    known = placed(known, 2, inner(w0, y0))
    known = placed(known, 3, inner(r0, y0))
    known = placed(known, 4, inner(y0, q0))

    def summed(phase, total, source, slots, offsets):
        source[...] = total
        for place, distances in enumerate(offsets):
            pltpu.make_async_remote_copy(
                src_ref=source,
                dst_ref=slots.at[place],
                send_sem=send_sem.at[phase],
                recv_sem=recv_sem.at[phase],
                device_id=away(distances),
                device_id_type=MESH,
            ).start()
        arrived(phase, slots, len(offsets))
        return total + jnp.sum(slots[...], axis=0)

    plane = [(0, b, c) for b in range(sizes[1]) for c in range(sizes[2])][1:]
    ring = [(a, 0, 0) for a in range(1, sizes[0])]
    total = summed(6, known, parts, part_plane, plane)
    total = summed(7, total, sums_plane, part_ring, ring)

    row = lax.broadcasted_iota(jnp.int32, (SYS, BS), 0)
    rz0, c0, wy, ry, yq = (
        jnp.where(row == 0, total[:, 2 * i : 2 * i + 1], total[:, 2 * i + 1 : 2 * i + 2]) for i in range(SUMS)
    )
    alpha = rz0 / c0
    rz1 = rz0 - alpha * (ry + c0) + alpha * alpha * wy
    scale = 1.0 + rz1 / rz0
    c1 = scale * scale * c0 - 2.0 * alpha * scale * wy + alpha * alpha * yq
    alpha1 = rz1 / c1
    charges[...] = alpha * z0 + alpha1 * (scale * z0 - alpha * y0)
    resid[...] = r0 - alpha * w0 - alpha1 * (scale * w0 - alpha * q0)
    for phase, target in ((0, halo_a), (1, fold_b), (2, both_c), (3, halo_d), (4, fold_e), (5, both_f)):
        left(phase, target, CODES - 1)
    for phase, target in ((6, part_plane), (7, part_ring)):
        left(phase, target, target.shape[0])


def finish(charges, residual, charges_out, residual_out, sem):
    copies = [
        pltpu.make_async_copy(charges, charges_out, sem.at[0]),
        pltpu.make_async_copy(residual, residual_out, sem.at[1]),
    ]
    for copy in copies:
        copy.start()
    for copy in copies:
        copy.wait()


def body(sizes, right_side, hardness, coupling, coupling_cols, coupling_count, precond_diag, precond, precond_cols):
    f32, i32, bf16 = jnp.float32, jnp.int32, jnp.bfloat16
    vec = jax.ShapeDtypeStruct((SYS, BS), f32)
    slots = lambda n, rows=SYS: pltpu.VMEM((n, rows, BS), f32)
    anywhere = pl.BlockSpec(memory_space=pl.ANY)

    def run(*refs):
        kernel(sizes, *refs)

    charges, residual = pl.pallas_call(
        run,
        out_shape=(pltpu.VMEM((SYS, BS), f32),) * 2,
        in_specs=[anywhere] * 8,
        out_specs=(pl.BlockSpec(memory_space=pltpu.VMEM),)*2,
        scratch_shapes=[
            pltpu.VMEM((SYS, BS), f32), pltpu.VMEM((1, BS), f32), pltpu.VMEM((SLOTS, BS, BS), bf16),
            pltpu.VMEM((1, BS), f32), pltpu.VMEM((SLOTS, BS, BS), bf16),
            pltpu.SMEM((1, SLOTS), i32), pltpu.SMEM((1, 1, 1), i32), pltpu.SMEM((1, SLOTS), i32),
            pltpu.SMEM((CODES,), i32), pltpu.SMEM((CODES,), i32), pltpu.SMEM((SLOTS,), i32),
            slots(CODES), slots(CODES), slots(CODES), slots(CODES, 2 * SYS), slots(CODES + 1, 2 * SYS),
            pltpu.VMEM((SYS, BS), f32), slots(CODES), slots(CODES), slots(CODES), slots(CODES, 2 * SYS), slots(CODES + 1, 2 * SYS),
            pltpu.VMEM((1, 128), f32), pltpu.VMEM((sizes[1] * sizes[2] - 1, 1, 128), f32),
            pltpu.VMEM((sizes[0] - 1, 1, 128), f32), pltpu.VMEM((1, 128), f32),
            slots(SLOTS + 1),
            pltpu.SemaphoreType.DMA((8,)), pltpu.SemaphoreType.DMA((8,)), pltpu.SemaphoreType.DMA((8,)),
        ],
        compiler_params=pltpu.CompilerParams(
            collective_id=0, has_side_effects=True, vmem_limit_bytes=56 * 1024 * 1024
        ),
    )(
        right_side.reshape(SYS, BS), hardness.reshape(1, BS), coupling.reshape(SLOTS, BS, BS),
        coupling_cols.reshape(1, SLOTS), coupling_count, precond_diag.reshape(1, BS),
        precond.reshape(SLOTS, BS, BS), precond_cols.reshape(1, SLOTS),
    )
    charges, residual = pl.pallas_call(
        finish,
        out_shape=(vec, vec),
        in_specs=[anywhere] * 2,
        out_specs=(anywhere, anywhere),
        scratch_shapes=[pltpu.SemaphoreType.DMA((2,))],
    )(charges, residual)
    return charges.reshape(right_side.shape), residual.reshape(right_side.shape)


def solution(mesh):
    sizes = tuple(mesh.shape[a] for a in AXES)
    placed = (
        P("gx", "gy", "gz", None, None),
        P("gx", "gy", "gz", None),
        P("gx", "gy", "gz", None, None, None),
        P("gx", "gy", "gz", None),
        P("gx", "gy", "gz"),
        P("gx", "gy", "gz", None),
        P("gx", "gy", "gz", None, None, None),
        P("gx", "gy", "gz", None),
    )
    return jax.shard_map(
        lambda *args: body(sizes, *args),
        mesh=mesh,
        in_specs=placed,
        out_specs=(P("gx", "gy", "gz", None, None), P("gx", "gy", "gz", None, None)),
        check_vma=False,
    )
```

```python
import jax
import jax.numpy as jnp
from jax import lax
from jax.experimental import pallas as pl
from jax.experimental.pallas import tpu as pltpu
from jax.sharding import PartitionSpec as P

SYS = 2
BS = 256
SLOTS = 6
CODES = 27
SELF = 13
AXES = ("gx", "gy", "gz")
MESH = pl.DeviceIdType.MESH
NEAR = sorted(
    (o for o in range(CODES) if o != SELF),
    key=lambda o: -(abs(o // 9 - 1) + abs(o // 3 % 3 - 1) + abs(o % 3 - 1)),
)


FURTHER = ((-2, 0, 0), (2, 0, 0), (0, 0, -2), (0, 0, 2))
SUMS = 5


def two_parts(vec):
    rest = vec - vec.astype(jnp.bfloat16).astype(jnp.float32)
    return jnp.concatenate([vec, rest], axis=0).astype(jnp.bfloat16)


def joined(product):
    return product[0:SYS] + product[SYS : 2 * SYS]


def tree_sum(terms):
    while len(terms) > 1:
        half = len(terms) // 2
        terms = [a + b for a, b in zip(terms[:half], terms[half : 2 * half])] + terms[2 * half :]
    return terms[0]


def dot_fwd(vec, tile):
    return lax.dot_general(vec, tile, (((1,), (1,)), ((), ())), preferred_element_type=jnp.float32)


def dot_bwd(vec, tile):
    return lax.dot_general(vec, tile, (((1,), (0,)), ((), ())), preferred_element_type=jnp.float32)


def kernel(
    sizes,
    rhs_hbm, hard_hbm, coup_hbm, ccol_hbm, ccnt_hbm, pdia_hbm, prec_hbm, pcol_hbm,
    charges, resid,
    rhs, hard, coup, pdia, prec, ccol, ccnt, pcol,
    inv_g, inv_h, sel_h,
    halo_a, send_b, fold_b, send_c, both_c, send_d, halo_d, send_e, fold_e, send_f, both_f,
    parts, part_plane, part_ring, sums_plane,
    terms,
    load_sem, send_sem, recv_sem,
):
    me = [lax.axis_index(a) for a in AXES]
    steps = [
        [lax.rem(me[a] + (n - 1), n), me[a], lax.rem(me[a] + 1, n)] for a, n in enumerate(sizes)
    ]

    def near(code):
        return (steps[0][code // 9], steps[1][code // 3 % 3], steps[2][code % 3])

    def away(distances):
        return tuple(
            m if d == 0 else lax.rem(m + d % n, n) for m, d, n in zip(me, distances, sizes)
        )

    loads = [
        pltpu.make_async_copy(source, target, load_sem.at[i])
        for i, (source, target) in enumerate((
            (rhs_hbm, rhs), (pcol_hbm, pcol), (ccol_hbm, ccol), (ccnt_hbm, ccnt), (pdia_hbm, pdia),
            (prec_hbm, prec), (hard_hbm, hard), (coup_hbm, coup),
        ))
    ]

    barrier = pltpu.get_barrier_semaphore()
    for code in NEAR:
        pl.semaphore_signal(barrier, inc=1, device_id=near(code), device_id_type=MESH)
    for distances in FURTHER:
        pl.semaphore_signal(barrier, inc=1, device_id=away(distances), device_id_type=MESH)
    for load in loads:
        load.start()

    zero = jnp.zeros((SYS, BS), jnp.float32)
    terms[SLOTS] = zero
    both_c[CODES, 0:SYS] = zero
    both_f[CODES, 0:SYS] = zero

    loads[0].wait()
    halo_a[SELF] = rhs[...]
    pl.semaphore_wait(barrier, len(NEAR) + len(FURTHER))

    def exchange(phase, source_of, target):
        for code in NEAR:
            pltpu.make_async_remote_copy(
                src_ref=source_of(code),
                dst_ref=target.at[CODES - 1 - code],
                send_sem=send_sem.at[phase],
                recv_sem=recv_sem.at[phase],
                device_id=near(code),
                device_id_type=MESH,
            ).start()

    def arrived(phase, target, n):
        here = target.at[pl.ds(0, n)]
        pltpu.make_async_copy(here, here, recv_sem.at[phase]).wait()

    def left(phase, target, n):
        here = target.at[pl.ds(0, n)]
        pltpu.make_async_copy(here, here, send_sem.at[phase]).wait()

    def forward(tiles, codes, halo, rows):
        total = None
        for k in range(SLOTS):
            picked = halo[SELF, rows] if k == 0 else halo[codes[k], rows]
            term = dot_fwd(two_parts(picked), tiles[k])
            total = term if total is None else total + term
        return joined(total)

    def backward(tiles, vec):
        pair = two_parts(vec)
        for k in range(1, SLOTS):
            terms[k] = joined(dot_bwd(pair, tiles[k]))
        return joined(dot_bwd(pair, tiles[0]))

    def folded(fold, rows):
        return tree_sum([fold[code, rows] for code in NEAR])

    def inner(left_vec, right_vec):
        return jnp.sum(left_vec * right_vec, axis=1, keepdims=True)

    everything = slice(0, SYS)
    second = slice(SYS, 2 * SYS)

    def apply_m_tail(vec, halo, send, fold, phase):
        inter = pdia[...] * vec + forward(prec, codes_g, halo, everything)
        own = backward(prec, inter)
        for code in NEAR:
            send[code] = terms[inv_g[code]]
        exchange(phase, lambda code: send.at[code], fold)
        partial = pdia[...] * inter + own
        arrived(phase, fold, CODES - 1)
        return partial + folded(fold, everything)

    def apply_h_start(vec, send, both, phase):
        own = backward(coup, vec)
        for code in NEAR:
            send[code, everything] = vec
            send[code, second] = terms[inv_h[code]]
        exchange(phase, lambda code: send.at[code], both)
        both[SELF, everything] = vec
        return own

    def apply_h(vec, send, both, phase):
        own = apply_h_start(vec, send, both, phase)
        partial = hard[...] * vec + own
        arrived(phase, both, CODES - 1)
        return partial + folded(both, second) + forward(coup, codes_h, both, everything)

    r0 = rhs[...]
    exchange(0, lambda code: rhs, halo_a)
    for load in loads[1:4]:
        load.wait()
    codes_g = [pcol[0, k] for k in range(SLOTS)]
    count = ccnt[0, 0, 0]
    codes_h = [ccol[0, k] for k in range(SLOTS)]
    for k in range(SLOTS):
        sel_h[k] = jnp.where(k < count, codes_h[k], CODES)
    codes_h = [sel_h[k] for k in range(SLOTS)]
    for inv, codes in ((inv_g, codes_g), (inv_h, codes_h)):
        for code in NEAR:
            slot = jnp.int32(SLOTS)
            for k in range(1, SLOTS):
                slot = jnp.where(codes[k] == code, k, slot)
            inv[code] = slot

    for load in loads[4:6]:
        load.wait()
    arrived(0, halo_a, CODES - 1)
    z0 = apply_m_tail(r0, halo_a, send_b, fold_b, 1)
    for load in loads[6:]:
        load.wait()
    w0 = apply_h(z0, send_c, both_c, 2)
    send_d[...] = w0
    halo_d[SELF] = w0
    exchange(3, lambda code: send_d, halo_d)
    lane = lax.broadcasted_iota(jnp.int32, (1, 128), 1)

    def placed(row, place, value):
        row = jnp.where(lane == 2 * place, value[0:1], row)
        return jnp.where(lane == 2 * place + 1, value[1:2], row)

    known = placed(jnp.zeros((1, 128), jnp.float32), 0, inner(r0, z0))
    known = placed(known, 1, inner(z0, w0))
    arrived(3, halo_d, CODES - 1)
    y0 = apply_m_tail(w0, halo_d, send_e, fold_e, 4)
    own = apply_h_start(y0, send_f, both_f, 5)
    known = placed(known, 2, inner(w0, y0))
    known = placed(known, 3, inner(r0, y0))
    scaled = hard[...] * y0
    arrived(5, both_f, CODES - 1)
    back = own + folded(both_f, second)
    known = placed(known, 4, inner(y0, scaled + 2.0 * back))

    def spread(phase, total, source, slots, offsets):
        source[...] = total
        for place, distances in enumerate(offsets):
            pltpu.make_async_remote_copy(
                src_ref=source,
                dst_ref=slots.at[place],
                send_sem=send_sem.at[phase],
                recv_sem=recv_sem.at[phase],
                device_id=away(distances),
                device_id_type=MESH,
            ).start()

    def summed(phase, total, slots, offsets):
        arrived(phase, slots, len(offsets))
        return tree_sum([total] + [slots[place] for place in range(len(offsets))])

    plane = [(0, b, c) for b in range(sizes[1]) for c in range(sizes[2])][1:]
    ring = [(a, 0, 0) for a in range(1, sizes[0])]
    spread(6, known, parts, part_plane, plane)
    q0 = scaled + back + forward(coup, codes_h, both_f, everything)
    total = summed(6, known, part_plane, plane)
    spread(7, total, sums_plane, part_ring, ring)
    for phase, target in ((0, halo_a), (1, fold_b), (2, both_c), (3, halo_d), (4, fold_e), (5, both_f)):
        left(phase, target, CODES - 1)
    left(6, part_plane, len(plane))
    total = summed(7, total, part_ring, ring)

    row = lax.broadcasted_iota(jnp.int32, (SYS, BS), 0)
    rz0, c0, wy, ry, yq = (
        jnp.where(row == 0, total[:, 2 * i : 2 * i + 1], total[:, 2 * i + 1 : 2 * i + 2]) for i in range(SUMS)
    )
    alpha = rz0 / c0
    rz1 = rz0 - alpha * (ry + c0) + alpha * alpha * wy
    scale = 1.0 + rz1 / rz0
    c1 = scale * scale * c0 - 2.0 * alpha * scale * wy + alpha * alpha * yq
    alpha1 = rz1 / c1
    charges[...] = alpha * z0 + alpha1 * (scale * z0 - alpha * y0)
    resid[...] = r0 - alpha * w0 - alpha1 * (scale * w0 - alpha * q0)
    left(7, part_ring, len(ring))


def finish(charges, residual, charges_out, residual_out, sem):
    copies = [
        pltpu.make_async_copy(charges, charges_out, sem.at[0]),
        pltpu.make_async_copy(residual, residual_out, sem.at[1]),
    ]
    for copy in copies:
        copy.start()
    for copy in copies:
        copy.wait()


def body(sizes, right_side, hardness, coupling, coupling_cols, coupling_count, precond_diag, precond, precond_cols):
    f32, i32, bf16 = jnp.float32, jnp.int32, jnp.bfloat16
    vec = jax.ShapeDtypeStruct((SYS, BS), f32)
    slots = lambda n, rows=SYS: pltpu.VMEM((n, rows, BS), f32)
    anywhere = pl.BlockSpec(memory_space=pl.ANY)

    def run(*refs):
        kernel(sizes, *refs)

    charges, residual = pl.pallas_call(
        run,
        out_shape=(pltpu.VMEM((SYS, BS), f32),) * 2,
        in_specs=[anywhere] * 8,
        out_specs=(pl.BlockSpec(memory_space=pltpu.VMEM),) * 2,
        scratch_shapes=[
            pltpu.VMEM((SYS, BS), f32), pltpu.VMEM((1, BS), f32), pltpu.VMEM((SLOTS, BS, BS), bf16),
            pltpu.VMEM((1, BS), f32), pltpu.VMEM((SLOTS, BS, BS), bf16),
            pltpu.SMEM((1, SLOTS), i32), pltpu.SMEM((1, 1, 1), i32), pltpu.SMEM((1, SLOTS), i32),
            pltpu.SMEM((CODES,), i32), pltpu.SMEM((CODES,), i32), pltpu.SMEM((SLOTS,), i32),
            slots(CODES), slots(CODES), slots(CODES), slots(CODES, 2 * SYS), slots(CODES + 1, 2 * SYS),
            pltpu.VMEM((SYS, BS), f32), slots(CODES), slots(CODES), slots(CODES), slots(CODES, 2 * SYS), slots(CODES + 1, 2 * SYS),
            pltpu.VMEM((1, 128), f32), pltpu.VMEM((sizes[1] * sizes[2] - 1, 1, 128), f32),
            pltpu.VMEM((sizes[0] - 1, 1, 128), f32), pltpu.VMEM((1, 128), f32),
            slots(SLOTS + 1),
            pltpu.SemaphoreType.DMA((8,)), pltpu.SemaphoreType.DMA((8,)), pltpu.SemaphoreType.DMA((8,)),
        ],
        compiler_params=pltpu.CompilerParams(
            collective_id=0, has_side_effects=True, vmem_limit_bytes=56 * 1024 * 1024
        ),
    )(
        right_side.reshape(SYS, BS), hardness.reshape(1, BS), coupling.reshape(SLOTS, BS, BS),
        coupling_cols.reshape(1, SLOTS), coupling_count, precond_diag.reshape(1, BS),
        precond.reshape(SLOTS, BS, BS), precond_cols.reshape(1, SLOTS),
    )
    charges, residual = pl.pallas_call(
        finish,
        out_shape=(vec, vec),
        in_specs=[anywhere] * 2,
        out_specs=(anywhere, anywhere),
        scratch_shapes=[pltpu.SemaphoreType.DMA((2,))],
        compiler_params=pltpu.CompilerParams(vmem_limit_bytes=1024 * 1024),
    )(charges, residual)
    return charges.reshape(right_side.shape), residual.reshape(right_side.shape)


def solution(mesh):
    sizes = tuple(mesh.shape[a] for a in AXES)
    placed = (
        P("gx", "gy", "gz", None, None),
        P("gx", "gy", "gz", None),
        P("gx", "gy", "gz", None, None, None),
        P("gx", "gy", "gz", None),
        P("gx", "gy", "gz"),
        P("gx", "gy", "gz", None),
        P("gx", "gy", "gz", None, None, None),
        P("gx", "gy", "gz", None),
    )
    return jax.shard_map(
        lambda *args: body(sizes, *args),
        mesh=mesh,
        in_specs=placed,
        out_specs=(P("gx", "gy", "gz", None, None), P("gx", "gy", "gz", None, None)),
        check_vma=False,
    )
```

```python
import jax
import jax.numpy as jnp
from jax import lax
from jax.experimental import pallas as pl
from jax.experimental.pallas import tpu as pltpu
from jax.sharding import PartitionSpec as P

SYS = 2
BS = 256
SLOTS = 6
CODES = 27
SELF = 13
AXES = ("gx", "gy", "gz")
MESH = pl.DeviceIdType.MESH
NEAR = sorted(
    (o for o in range(CODES) if o != SELF),
    key=lambda o: -(abs(o // 9 - 1) + abs(o // 3 % 3 - 1) + abs(o % 3 - 1)),
)


FURTHER = ((-2, 0, 0), (2, 0, 0), (0, 0, -2), (0, 0, 2))
SUMS = 5


def two_parts(vec):
    rest = vec - vec.astype(jnp.bfloat16).astype(jnp.float32)
    return jnp.concatenate([vec, rest], axis=0).astype(jnp.bfloat16)


def joined(product):
    return product[0:SYS] + product[SYS : 2 * SYS]


def tree_sum(terms):
    while len(terms) > 1:
        half = len(terms) // 2
        terms = [a + b for a, b in zip(terms[:half], terms[half : 2 * half])] + terms[2 * half :]
    return terms[0]


def dot(vec, tile):
    return lax.dot_general(vec, tile, (((1,), (0,)), ((), ())), preferred_element_type=jnp.float32)


def kernel(
    sizes,
    rhs_hbm, hard_hbm, coup_hbm, ccol_hbm, ccnt_hbm, pdia_hbm, prec_hbm, pcol_hbm,
    charges, resid,
    rhs, hard, coup, pdia, prec, ccol, ccnt, pcol,
    inv_g, inv_h, sel_h,
    halo_a, send_b, fold_b, send_c, both_c, send_d, halo_d, send_e, fold_e, send_f, both_f,
    parts, part_plane, part_ring, sums_plane,
    terms, coup_t, prec_t,
    load_sem, send_sem, recv_sem,
):
    me = [lax.axis_index(a) for a in AXES]
    steps = [
        [lax.rem(me[a] + (n - 1), n), me[a], lax.rem(me[a] + 1, n)] for a, n in enumerate(sizes)
    ]

    def near(code):
        return (steps[0][code // 9], steps[1][code // 3 % 3], steps[2][code % 3])

    def away(distances):
        return tuple(
            m if d == 0 else lax.rem(m + d % n, n) for m, d, n in zip(me, distances, sizes)
        )

    loads = [
        pltpu.make_async_copy(source, target, load_sem.at[i])
        for i, (source, target) in enumerate((
            (rhs_hbm, rhs), (pcol_hbm, pcol), (ccol_hbm, ccol), (ccnt_hbm, ccnt), (pdia_hbm, pdia),
            (prec_hbm, prec), (hard_hbm, hard), (coup_hbm, coup),
        ))
    ]

    barrier = pltpu.get_barrier_semaphore()
    for code in NEAR:
        pl.semaphore_signal(barrier, inc=1, device_id=near(code), device_id_type=MESH)
    for distances in FURTHER:
        pl.semaphore_signal(barrier, inc=1, device_id=away(distances), device_id_type=MESH)
    for load in loads:
        load.start()

    zero = jnp.zeros((SYS, BS), jnp.float32)
    terms[SLOTS] = zero
    both_c[CODES, 0:SYS] = zero
    both_f[CODES, 0:SYS] = zero

    loads[0].wait()
    halo_a[SELF] = rhs[...]
    pl.semaphore_wait(barrier, len(NEAR) + len(FURTHER))

    def exchange(phase, source_of, target):
        for code in NEAR:
            pltpu.make_async_remote_copy(
                src_ref=source_of(code),
                dst_ref=target.at[CODES - 1 - code],
                send_sem=send_sem.at[phase],
                recv_sem=recv_sem.at[phase],
                device_id=near(code),
                device_id_type=MESH,
            ).start()

    def arrived(phase, target, n):
        here = target.at[pl.ds(0, n)]
        pltpu.make_async_copy(here, here, recv_sem.at[phase]).wait()

    def left(phase, target, n):
        here = target.at[pl.ds(0, n)]
        pltpu.make_async_copy(here, here, send_sem.at[phase]).wait()

    def turn(tiles, turned):
        for k in range(SLOTS):
            turned[k] = tiles[k].T

    def forward(turned, codes, halo, rows):
        total = None
        for k in range(SLOTS):
            picked = halo[SELF, rows] if k == 0 else halo[codes[k], rows]
            term = dot(two_parts(picked), turned[k])
            total = term if total is None else total + term
        return joined(total)

    def backward(tiles, vec):
        pair = two_parts(vec)
        for k in range(1, SLOTS):
            terms[k] = joined(dot(pair, tiles[k]))
        return joined(dot(pair, tiles[0]))

    def folded(fold, rows):
        return tree_sum([fold[code, rows] for code in NEAR])

    def inner(left_vec, right_vec):
        return jnp.sum(left_vec * right_vec, axis=1, keepdims=True)

    everything = slice(0, SYS)
    second = slice(SYS, 2 * SYS)

    def apply_m_tail(vec, halo, send, fold, phase, meanwhile=None):
        inter = pdia[...] * vec + forward(prec_t, codes_g, halo, everything)
        own = backward(prec, inter)
        for code in NEAR:
            send[code] = terms[inv_g[code]]
        exchange(phase, lambda code: send.at[code], fold)
        partial = pdia[...] * inter + own
        if meanwhile is not None:
            meanwhile()
        arrived(phase, fold, CODES - 1)
        return partial + folded(fold, everything)

    def apply_h_start(vec, send, both, phase):
        own = backward(coup, vec)
        for code in NEAR:
            send[code, everything] = vec
            send[code, second] = terms[inv_h[code]]
        exchange(phase, lambda code: send.at[code], both)
        both[SELF, everything] = vec
        return own

    def apply_h(vec, send, both, phase):
        own = apply_h_start(vec, send, both, phase)
        partial = hard[...] * vec + own
        arrived(phase, both, CODES - 1)
        return partial + folded(both, second) + forward(coup_t, codes_h, both, everything)

    r0 = rhs[...]
    exchange(0, lambda code: rhs, halo_a)
    for load in loads[1:4]:
        load.wait()
    codes_g = [pcol[0, k] for k in range(SLOTS)]
    count = ccnt[0, 0, 0]
    codes_h = [ccol[0, k] for k in range(SLOTS)]
    for k in range(SLOTS):
        sel_h[k] = jnp.where(k < count, codes_h[k], CODES)
    codes_h = [sel_h[k] for k in range(SLOTS)]
    for inv, codes in ((inv_g, codes_g), (inv_h, codes_h)):
        for code in NEAR:
            slot = jnp.int32(SLOTS)
            for k in range(1, SLOTS):
                slot = jnp.where(codes[k] == code, k, slot)
            inv[code] = slot

    for load in loads[4:6]:
        load.wait()
    turn(prec, prec_t)
    arrived(0, halo_a, CODES - 1)

    def ready_coupling():
        for load in loads[6:]:
            load.wait()
        turn(coup, coup_t)

    z0 = apply_m_tail(r0, halo_a, send_b, fold_b, 1, ready_coupling)
    w0 = apply_h(z0, send_c, both_c, 2)
    send_d[...] = w0
    halo_d[SELF] = w0
    exchange(3, lambda code: send_d, halo_d)
    lane = lax.broadcasted_iota(jnp.int32, (1, 128), 1)

    def placed(row, place, value):
        row = jnp.where(lane == 2 * place, value[0:1], row)
        return jnp.where(lane == 2 * place + 1, value[1:2], row)

    known = placed(jnp.zeros((1, 128), jnp.float32), 0, inner(r0, z0))
    known = placed(known, 1, inner(z0, w0))
    arrived(3, halo_d, CODES - 1)
    y0 = apply_m_tail(w0, halo_d, send_e, fold_e, 4)
    own = apply_h_start(y0, send_f, both_f, 5)
    known = placed(known, 2, inner(w0, y0))
    known = placed(known, 3, inner(r0, y0))
    scaled = hard[...] * y0
    arrived(5, both_f, CODES - 1)
    back = own + folded(both_f, second)
    known = placed(known, 4, inner(y0, scaled + 2.0 * back))

    def spread(phase, total, source, slots, offsets):
        source[...] = total
        for place, distances in enumerate(offsets):
            pltpu.make_async_remote_copy(
                src_ref=source,
                dst_ref=slots.at[place],
                send_sem=send_sem.at[phase],
                recv_sem=recv_sem.at[phase],
                device_id=away(distances),
                device_id_type=MESH,
            ).start()

    def summed(phase, total, slots, offsets):
        arrived(phase, slots, len(offsets))
        return tree_sum([total] + [slots[place] for place in range(len(offsets))])

    def hops(distances):
        x, y, z = (min(d, n - d) for d, n in zip(distances, sizes))
        return -(x + y + z / 2)

    plane = sorted([(0, b, c) for b in range(sizes[1]) for c in range(sizes[2])][1:], key=hops)
    ring = sorted([(a, 0, 0) for a in range(1, sizes[0])], key=hops)
    spread(6, known, parts, part_plane, plane)
    q0 = scaled + back + forward(coup_t, codes_h, both_f, everything)
    total = summed(6, known, part_plane, plane)
    spread(7, total, sums_plane, part_ring, ring)
    for phase, target in ((0, halo_a), (1, fold_b), (2, both_c), (3, halo_d), (4, fold_e), (5, both_f)):
        left(phase, target, CODES - 1)
    left(6, part_plane, len(plane))
    total = summed(7, total, part_ring, ring)

    row = lax.broadcasted_iota(jnp.int32, (SYS, BS), 0)
    rz0, c0, wy, ry, yq = (
        jnp.where(row == 0, total[:, 2 * i : 2 * i + 1], total[:, 2 * i + 1 : 2 * i + 2]) for i in range(SUMS)
    )
    alpha = rz0 / c0
    rz1 = rz0 - alpha * (ry + c0) + alpha * alpha * wy
    scale = 1.0 + rz1 / rz0
    c1 = scale * scale * c0 - 2.0 * alpha * scale * wy + alpha * alpha * yq
    alpha1 = rz1 / c1
    charges[...] = alpha * z0 + alpha1 * (scale * z0 - alpha * y0)
    resid[...] = r0 - alpha * w0 - alpha1 * (scale * w0 - alpha * q0)
    left(7, part_ring, len(ring))


def finish(charges, residual, charges_out, residual_out, sem):
    copies = [
        pltpu.make_async_copy(charges, charges_out, sem.at[0]),
        pltpu.make_async_copy(residual, residual_out, sem.at[1]),
    ]
    for copy in copies:
        copy.start()
    for copy in copies:
        copy.wait()


def body(sizes, right_side, hardness, coupling, coupling_cols, coupling_count, precond_diag, precond, precond_cols):
    f32, i32, bf16 = jnp.float32, jnp.int32, jnp.bfloat16
    vec = jax.ShapeDtypeStruct((SYS, BS), f32)
    slots = lambda n, rows=SYS: pltpu.VMEM((n, rows, BS), f32)
    anywhere = pl.BlockSpec(memory_space=pl.ANY)

    def run(*refs):
        kernel(sizes, *refs)

    charges, residual = pl.pallas_call(
        run,
        out_shape=(pltpu.VMEM((SYS, BS), f32),) * 2,
        in_specs=[anywhere] * 8,
        out_specs=(pl.BlockSpec(memory_space=pltpu.VMEM),) * 2,
        scratch_shapes=[
            pltpu.VMEM((SYS, BS), f32), pltpu.VMEM((1, BS), f32), pltpu.VMEM((SLOTS, BS, BS), bf16),
            pltpu.VMEM((1, BS), f32), pltpu.VMEM((SLOTS, BS, BS), bf16),
            pltpu.SMEM((1, SLOTS), i32), pltpu.SMEM((1, 1, 1), i32), pltpu.SMEM((1, SLOTS), i32),
            pltpu.SMEM((CODES,), i32), pltpu.SMEM((CODES,), i32), pltpu.SMEM((SLOTS,), i32),
            slots(CODES), slots(CODES), slots(CODES), slots(CODES, 2 * SYS), slots(CODES + 1, 2 * SYS),
            pltpu.VMEM((SYS, BS), f32), slots(CODES), slots(CODES), slots(CODES), slots(CODES, 2 * SYS), slots(CODES + 1, 2 * SYS),
            pltpu.VMEM((1, 128), f32), pltpu.VMEM((sizes[1] * sizes[2] - 1, 1, 128), f32),
            pltpu.VMEM((sizes[0] - 1, 1, 128), f32), pltpu.VMEM((1, 128), f32),
            slots(SLOTS + 1), pltpu.VMEM((SLOTS, BS, BS), bf16), pltpu.VMEM((SLOTS, BS, BS), bf16),
            pltpu.SemaphoreType.DMA((8,)), pltpu.SemaphoreType.DMA((8,)), pltpu.SemaphoreType.DMA((8,)),
        ],
        compiler_params=pltpu.CompilerParams(
            collective_id=0, has_side_effects=True, vmem_limit_bytes=56 * 1024 * 1024
        ),
    )(
        right_side.reshape(SYS, BS), hardness.reshape(1, BS), coupling.reshape(SLOTS, BS, BS),
        coupling_cols.reshape(1, SLOTS), coupling_count, precond_diag.reshape(1, BS),
        precond.reshape(SLOTS, BS, BS), precond_cols.reshape(1, SLOTS),
    )
    charges, residual = pl.pallas_call(
        finish,
        out_shape=(vec, vec),
        in_specs=[anywhere] * 2,
        out_specs=(anywhere, anywhere),
        scratch_shapes=[pltpu.SemaphoreType.DMA((2,))],
        compiler_params=pltpu.CompilerParams(vmem_limit_bytes=1024 * 1024),
    )(charges, residual)
    return charges.reshape(right_side.shape), residual.reshape(right_side.shape)


def solution(mesh):
    sizes = tuple(mesh.shape[a] for a in AXES)
    placed = (
        P("gx", "gy", "gz", None, None),
        P("gx", "gy", "gz", None),
        P("gx", "gy", "gz", None, None, None),
        P("gx", "gy", "gz", None),
        P("gx", "gy", "gz"),
        P("gx", "gy", "gz", None),
        P("gx", "gy", "gz", None, None, None),
        P("gx", "gy", "gz", None),
    )
    return jax.shard_map(
        lambda *args: body(sizes, *args),
        mesh=mesh,
        in_specs=placed,
        out_specs=(P("gx", "gy", "gz", None, None), P("gx", "gy", "gz", None, None)),
        check_vma=False,
    )
```

```python
import jax
import jax.numpy as jnp
from jax import lax
from jax.experimental import pallas as pl
from jax.experimental.pallas import tpu as pltpu
from jax.sharding import PartitionSpec as P

SYS = 2
BS = 256
SLOTS = 6
CODES = 27
SELF = 13
AXES = ("gx", "gy", "gz")
MESH = pl.DeviceIdType.MESH
OVER, BESIDE = 1, 2
NEAR = sorted(
    ((x, y, t) for x in (-1, 0, 1) for y in (-1, 0, 1) for t in (0, OVER, BESIDE) if (x, y, t) != (0, 0, 0)),
    key=lambda o: -(4 * (abs(o[0]) + abs(o[1]) + (o[2] == OVER)) + (o[2] == BESIDE)),
)
FURTHER = ((-2, 0, 0), (2, 0, 0), (0, 0, -2), (0, 0, 2))
SUMS = 5


def two_parts(vec):
    rest = vec - vec.astype(jnp.bfloat16).astype(jnp.float32)
    return jnp.concatenate([vec, rest], axis=0).astype(jnp.bfloat16)


def joined(product):
    return product[0:SYS] + product[SYS : 2 * SYS]


def tree_sum(terms):
    while len(terms) > 1:
        half = len(terms) // 2
        terms = [a + b for a, b in zip(terms[:half], terms[half : 2 * half])] + terms[2 * half :]
    return terms[0]


def dot(vec, tile):
    return lax.dot_general(vec, tile, (((1,), (0,)), ((), ())), preferred_element_type=jnp.float32)


def kernel(
    sizes,
    rhs_hbm, hard_hbm, coup_hbm, ccol_hbm, ccnt_hbm, pdia_hbm, prec_hbm, pcol_hbm,
    charges, resid,
    rhs, hard, coup, pdia, prec, ccol, ccnt, pcol,
    inv_g, inv_h, sel_h,
    halo_a, send_b, fold_b, send_c, both_c, send_d, halo_d, send_e, fold_e, send_f, both_f,
    parts, part_plane, part_ring, sums_plane,
    terms, coup_t, prec_t,
    load_sem, send_sem, recv_sem,
):
    me = [lax.axis_index(a) for a in AXES]
    steps = [
        [lax.rem(me[a] + (n - 1), n), me[a], lax.rem(me[a] + 1, n)] for a, n in enumerate(sizes)
    ]
    core = lax.rem(me[2], 2)
    thirds = [1, 2 * core, 2 - 2 * core]
    leads = [
        me[2],
        lax.rem(me[2] + (sizes[2] - 1) + 2 * core, sizes[2]),
        me[2] + 1 - 2 * core,
    ]

    def code_of(o):
        return (o[0] + 1) * 9 + (o[1] + 1) * 3 + thirds[o[2]]

    def near(o):
        return (steps[0][o[0] + 1], steps[1][o[1] + 1], leads[o[2]])

    def away(distances):
        return tuple(
            m if d == 0 else lax.rem(m + d % n, n) for m, d, n in zip(me, distances, sizes)
        )

    loads = [
        pltpu.make_async_copy(source, target, load_sem.at[i])
        for i, (source, target) in enumerate((
            (rhs_hbm, rhs), (pcol_hbm, pcol), (ccol_hbm, ccol), (ccnt_hbm, ccnt), (pdia_hbm, pdia),
            (prec_hbm, prec), (hard_hbm, hard), (coup_hbm, coup),
        ))
    ]

    barrier = pltpu.get_barrier_semaphore()
    for offset in NEAR:
        pl.semaphore_signal(barrier, inc=1, device_id=near(offset), device_id_type=MESH)
    for distances in FURTHER:
        pl.semaphore_signal(barrier, inc=1, device_id=away(distances), device_id_type=MESH)
    for load in loads:
        load.start()

    zero = jnp.zeros((SYS, BS), jnp.float32)
    terms[SLOTS] = zero
    both_c[CODES, 0:SYS] = zero
    both_f[CODES, 0:SYS] = zero

    loads[0].wait()
    halo_a[SELF] = rhs[...]
    pl.semaphore_wait(barrier, len(NEAR) + len(FURTHER))

    def exchange(phase, source_of, target):
        for offset in NEAR:
            code = code_of(offset)
            pltpu.make_async_remote_copy(
                src_ref=source_of(code),
                dst_ref=target.at[CODES - 1 - code],
                send_sem=send_sem.at[phase],
                recv_sem=recv_sem.at[phase],
                device_id=near(offset),
                device_id_type=MESH,
            ).start()

    def arrived(phase, target, n):
        here = target.at[pl.ds(0, n)]
        pltpu.make_async_copy(here, here, recv_sem.at[phase]).wait()

    def left(phase, target, n):
        here = target.at[pl.ds(0, n)]
        pltpu.make_async_copy(here, here, send_sem.at[phase]).wait()

    def turn(tiles, turned):
        for k in range(SLOTS):
            turned[k] = tiles[k].T

    def forward(turned, codes, halo, rows):
        total = None
        for k in range(SLOTS):
            picked = halo[SELF, rows] if k == 0 else halo[codes[k], rows]
            term = dot(two_parts(picked), turned[k])
            total = term if total is None else total + term
        return joined(total)

    def backward(tiles, vec):
        pair = two_parts(vec)
        for k in range(1, SLOTS):
            terms[k] = joined(dot(pair, tiles[k]))
        return joined(dot(pair, tiles[0]))

    def folded(fold, rows):
        return tree_sum([fold[code, rows] for code in range(CODES) if code != SELF])

    def inner(left_vec, right_vec):
        return jnp.sum(left_vec * right_vec, axis=1, keepdims=True)

    everything = slice(0, SYS)
    second = slice(SYS, 2 * SYS)

    def apply_m_tail(vec, halo, send, fold, phase, meanwhile=None):
        inter = pdia[...] * vec + forward(prec_t, codes_g, halo, everything)
        own = backward(prec, inter)
        for code in range(CODES):
            send[code] = terms[inv_g[code]]
        exchange(phase, lambda code: send.at[code], fold)
        partial = pdia[...] * inter + own
        if meanwhile is not None:
            meanwhile()
        arrived(phase, fold, CODES - 1)
        return partial + folded(fold, everything)

    def apply_h_start(vec, send, both, phase):
        own = backward(coup, vec)
        for code in range(CODES):
            send[code, everything] = vec
            send[code, second] = terms[inv_h[code]]
        exchange(phase, lambda code: send.at[code], both)
        both[SELF, everything] = vec
        return own

    def apply_h(vec, send, both, phase):
        own = apply_h_start(vec, send, both, phase)
        partial = hard[...] * vec + own
        arrived(phase, both, CODES - 1)
        return partial + folded(both, second) + forward(coup_t, codes_h, both, everything)

    r0 = rhs[...]
    exchange(0, lambda code: rhs, halo_a)
    for load in loads[1:4]:
        load.wait()
    codes_g = [pcol[0, k] for k in range(SLOTS)]
    count = ccnt[0, 0, 0]
    codes_h = [ccol[0, k] for k in range(SLOTS)]
    for k in range(SLOTS):
        sel_h[k] = jnp.where(k < count, codes_h[k], CODES)
    codes_h = [sel_h[k] for k in range(SLOTS)]
    for inv, codes in ((inv_g, codes_g), (inv_h, codes_h)):
        for code in range(CODES):
            slot = jnp.int32(SLOTS)
            for k in range(1, SLOTS):
                slot = jnp.where(codes[k] == code, k, slot)
            inv[code] = slot

    for load in loads[4:6]:
        load.wait()
    turn(prec, prec_t)
    arrived(0, halo_a, CODES - 1)

    def ready_coupling():
        for load in loads[6:]:
            load.wait()
        turn(coup, coup_t)

    z0 = apply_m_tail(r0, halo_a, send_b, fold_b, 1, ready_coupling)
    w0 = apply_h(z0, send_c, both_c, 2)
    send_d[...] = w0
    halo_d[SELF] = w0
    exchange(3, lambda code: send_d, halo_d)
    lane = lax.broadcasted_iota(jnp.int32, (1, 128), 1)

    def placed(row, place, value):
        row = jnp.where(lane == 2 * place, value[0:1], row)
        return jnp.where(lane == 2 * place + 1, value[1:2], row)

    known = placed(jnp.zeros((1, 128), jnp.float32), 0, inner(r0, z0))
    known = placed(known, 1, inner(z0, w0))
    arrived(3, halo_d, CODES - 1)
    y0 = apply_m_tail(w0, halo_d, send_e, fold_e, 4)
    own = apply_h_start(y0, send_f, both_f, 5)
    known = placed(known, 2, inner(w0, y0))
    known = placed(known, 3, inner(r0, y0))
    scaled = hard[...] * y0
    arrived(5, both_f, CODES - 1)
    back = own + folded(both_f, second)
    known = placed(known, 4, inner(y0, scaled + 2.0 * back))

    def spread(phase, total, source, slots, offsets):
        source[...] = total
        for place, distances in enumerate(offsets):
            pltpu.make_async_remote_copy(
                src_ref=source,
                dst_ref=slots.at[place],
                send_sem=send_sem.at[phase],
                recv_sem=recv_sem.at[phase],
                device_id=away(distances),
                device_id_type=MESH,
            ).start()

    def summed(phase, total, slots, offsets):
        arrived(phase, slots, len(offsets))
        return tree_sum([total] + [slots[place] for place in range(len(offsets))])

    def hops(distances):
        x, y, z = (min(d, n - d) for d, n in zip(distances, sizes))
        return -(x + y + z / 2)

    plane = sorted([(0, b, c) for b in range(sizes[1]) for c in range(sizes[2])][1:], key=hops)
    ring = sorted([(a, 0, 0) for a in range(1, sizes[0])], key=hops)
    spread(6, known, parts, part_plane, plane)
    q0 = scaled + back + forward(coup_t, codes_h, both_f, everything)
    total = summed(6, known, part_plane, plane)
    spread(7, total, sums_plane, part_ring, ring)
    for phase, target in ((0, halo_a), (1, fold_b), (2, both_c), (3, halo_d), (4, fold_e), (5, both_f)):
        left(phase, target, CODES - 1)
    left(6, part_plane, len(plane))
    total = summed(7, total, part_ring, ring)

    row = lax.broadcasted_iota(jnp.int32, (SYS, BS), 0)
    rz0, c0, wy, ry, yq = (
        jnp.where(row == 0, total[:, 2 * i : 2 * i + 1], total[:, 2 * i + 1 : 2 * i + 2]) for i in range(SUMS)
    )
    alpha = rz0 / c0
    rz1 = rz0 - alpha * (ry + c0) + alpha * alpha * wy
    scale = 1.0 + rz1 / rz0
    c1 = scale * scale * c0 - 2.0 * alpha * scale * wy + alpha * alpha * yq
    alpha1 = rz1 / c1
    charges[...] = alpha * z0 + alpha1 * (scale * z0 - alpha * y0)
    resid[...] = r0 - alpha * w0 - alpha1 * (scale * w0 - alpha * q0)
    left(7, part_ring, len(ring))


def finish(charges, residual, charges_out, residual_out, sem):
    copies = [
        pltpu.make_async_copy(charges, charges_out, sem.at[0]),
        pltpu.make_async_copy(residual, residual_out, sem.at[1]),
    ]
    for copy in copies:
        copy.start()
    for copy in copies:
        copy.wait()


def body(sizes, right_side, hardness, coupling, coupling_cols, coupling_count, precond_diag, precond, precond_cols):
    f32, i32, bf16 = jnp.float32, jnp.int32, jnp.bfloat16
    vec = jax.ShapeDtypeStruct((SYS, BS), f32)
    slots = lambda n, rows=SYS: pltpu.VMEM((n, rows, BS), f32)
    anywhere = pl.BlockSpec(memory_space=pl.ANY)

    def run(*refs):
        kernel(sizes, *refs)

    charges, residual = pl.pallas_call(
        run,
        out_shape=(pltpu.VMEM((SYS, BS), f32),) * 2,
        in_specs=[anywhere] * 8,
        out_specs=(pl.BlockSpec(memory_space=pltpu.VMEM),) * 2,
        scratch_shapes=[
            pltpu.VMEM((SYS, BS), f32), pltpu.VMEM((1, BS), f32), pltpu.VMEM((SLOTS, BS, BS), bf16),
            pltpu.VMEM((1, BS), f32), pltpu.VMEM((SLOTS, BS, BS), bf16),
            pltpu.SMEM((1, SLOTS), i32), pltpu.SMEM((1, 1, 1), i32), pltpu.SMEM((1, SLOTS), i32),
            pltpu.SMEM((CODES,), i32), pltpu.SMEM((CODES,), i32), pltpu.SMEM((SLOTS,), i32),
            slots(CODES), slots(CODES), slots(CODES), slots(CODES, 2 * SYS), slots(CODES + 1, 2 * SYS),
            pltpu.VMEM((SYS, BS), f32), slots(CODES), slots(CODES), slots(CODES), slots(CODES, 2 * SYS), slots(CODES + 1, 2 * SYS),
            pltpu.VMEM((1, 128), f32), pltpu.VMEM((sizes[1] * sizes[2] - 1, 1, 128), f32),
            pltpu.VMEM((sizes[0] - 1, 1, 128), f32), pltpu.VMEM((1, 128), f32),
            slots(SLOTS + 1), pltpu.VMEM((SLOTS, BS, BS), bf16), pltpu.VMEM((SLOTS, BS, BS), bf16),
            pltpu.SemaphoreType.DMA((8,)), pltpu.SemaphoreType.DMA((8,)), pltpu.SemaphoreType.DMA((8,)),
        ],
        compiler_params=pltpu.CompilerParams(
            collective_id=0, has_side_effects=True, vmem_limit_bytes=56 * 1024 * 1024
        ),
    )(
        right_side.reshape(SYS, BS), hardness.reshape(1, BS), coupling.reshape(SLOTS, BS, BS),
        coupling_cols.reshape(1, SLOTS), coupling_count, precond_diag.reshape(1, BS),
        precond.reshape(SLOTS, BS, BS), precond_cols.reshape(1, SLOTS),
    )
    charges, residual = pl.pallas_call(
        finish,
        out_shape=(vec, vec),
        in_specs=[anywhere] * 2,
        out_specs=(anywhere, anywhere),
        scratch_shapes=[pltpu.SemaphoreType.DMA((2,))],
        compiler_params=pltpu.CompilerParams(vmem_limit_bytes=1024 * 1024),
    )(charges, residual)
    return charges.reshape(right_side.shape), residual.reshape(right_side.shape)


def solution(mesh):
    sizes = tuple(mesh.shape[a] for a in AXES)
    placed = (
        P("gx", "gy", "gz", None, None),
        P("gx", "gy", "gz", None),
        P("gx", "gy", "gz", None, None, None),
        P("gx", "gy", "gz", None),
        P("gx", "gy", "gz"),
        P("gx", "gy", "gz", None),
        P("gx", "gy", "gz", None, None, None),
        P("gx", "gy", "gz", None),
    )
    return jax.shard_map(
        lambda *args: body(sizes, *args),
        mesh=mesh,
        in_specs=placed,
        out_specs=(P("gx", "gy", "gz", None, None), P("gx", "gy", "gz", None, None)),
        check_vma=False,
    )
```
